32 devices in a mesh: row: 2 (over x), col: 4 (over z), freq: 4 (over y, core).
Axes of the slice: x: 2, y: 2, z: 4, core: 2. Of those that a mesh axis runs over, the one named last changes fastest.
Arguments:
- traces: bfloat16 [24, 1024, 512], P(None, ('row', 'col'))
Outputs:
- correlation: float32 [1024, 2, 4, 128], P(('row', 'freq'), None, 'col')
All inputs are finite; a program needn't handle non-finite values.
Results may differ from the reference program's by a relative error of at most 0.0025.
Values may be sent and summed in bfloat16 or wider, within the bound.
A program may use at most 64 MiB of HBM per device.

```python
import math
import jax
import jax.numpy as jnp
from jax import lax

CH_DEV = 128
C = 1024
S = 512
FB = 256
W = 24
N_ROW = 2
N_COL = 4


def draw_traces(key, part):
    key = jax.random.fold_in(key, 7)
    keys = jax.random.split(key, 6)
    tones = jax.random.randint(keys[0], (4,), 1, max(S // 8, 2))
    amplitude = jax.random.uniform(keys[1], (4,), jnp.float32, 0.05, 0.25)
    moveout = jax.random.uniform(keys[2], (4,), jnp.float32, -0.05, 0.05)
    phases = jax.random.uniform(keys[3], (W, 4), jnp.float32, -math.pi, math.pi)
    times = jnp.arange(S, dtype=jnp.int32)
    places = jnp.arange(C, dtype=jnp.float32)
    coherent = jnp.zeros((W, C, S), jnp.float32)
    for tone in range(4):
        cycle = (tones[tone] * times % S).astype(jnp.float32) * (2.0 * math.pi / S)
        delay = places * moveout[tone] * tones[tone].astype(jnp.float32) * (2.0 * math.pi / S)
        angle = cycle[None, None, :] - delay[None, :, None] + phases[:, tone][:, None, None]
        coherent = coherent + amplitude[tone] * jnp.sin(angle)
    noise = jax.random.normal(keys[4], (W, C, S), jnp.float32)
    gains = jnp.exp(jax.random.uniform(keys[5], (C,), jnp.float32, math.log(0.3), math.log(3.0)))
    return (gains[None, :, None] * (noise + coherent)).astype(jnp.bfloat16)


def setup_inputs(seed: int = 0) -> dict:
    seeds = jax.random.split(jax.random.key(seed), 2)
    return {
        "traces": draw_traces(jax.random.fold_in(seeds[1], 71), 0),
    }


def reference(traces):
    signal = traces.astype(jnp.float32)
    windows = signal.shape[0]
    full = jnp.fft.rfft(signal, axis=-1)[:, :, 1:FB + 1]
    real_part = jnp.real(full).astype(jnp.float32)
    imag_part = jnp.imag(full).astype(jnp.float32)
    energy = lax.optimization_barrier(jnp.sum(real_part * real_part + imag_part * imag_part, axis=(0, 2)))
    inverse = lax.rsqrt(energy / (windows * 2 * FB) + 1e-05)
    whitened = jnp.concatenate([real_part, imag_part], axis=2) * inverse[None, :, None]
    whitened = whitened.astype(jnp.bfloat16).astype(jnp.float32)
    flat = jnp.transpose(whitened, (1, 0, 2)).reshape(C, windows * 2 * FB)
    total = jnp.dot(flat, flat.T, precision=lax.Precision.HIGHEST, preferred_element_type=jnp.float32)
    total = total / jnp.sqrt(jnp.float32(windows * 2 * FB))
    return total.reshape(C, N_ROW, N_COL, CH_DEV)
```

```python
import functools
import math

import jax
import jax.numpy as jnp
from jax import lax
from jax.experimental import pallas as pl
from jax.experimental.pallas import tpu as pltpu
from jax.sharding import PartitionSpec as P

MESH = pl.DeviceIdType.MESH
NT = (((1,), (1,)), ((), ()))


def kernel(
    n_row, n_col, n_freq, traces, out, spectra, blocks, whole, send_a, keep_a, recv_a, send_b, keep_b,
    recv_b, send_c, keep_c, recv_c, z_send, z_recv, x_send, x_recv, a_send, a_recv, b_send, b_recv,
    c_send, c_recv,
):
    windows, channels, samples = traces.shape
    part = samples // n_freq
    share = windows // n_col
    rows = n_col * channels // n_freq
    i, j, f = lax.axis_index("row"), lax.axis_index("col"), lax.axis_index("freq")
    core = lax.rem(f, 2)
    side = lax.div(f, 2)
    core_peer = (i, j, f + 1 - 2 * core)
    side_peer = (i, j, lax.rem(f + 2, n_freq))

    def col_peer(d):
        return (i, lax.rem(j + d, n_col), f)

    def row_peer(e):
        return (lax.rem(i + e, n_row), j, f)

    peers = [core_peer, side_peer]
    peers += [col_peer(d) for d in range(1, n_col)]
    peers += [row_peer(e) for e in range(1, n_row)]
    barrier = pltpu.get_barrier_semaphore()
    for peer in peers:
        pl.semaphore_signal(barrier, inc=1, device_id=peer, device_id_type=MESH)

    time = lax.broadcasted_iota(jnp.int32, (samples, 2 * part), 0)
    lane = lax.broadcasted_iota(jnp.int32, (samples, 2 * part), 1)
    odd = jnp.logical_and(lane >= part, lax.rem(time + lane, 2) == 1)
    table = jnp.where(odd, -1.0 / samples, 1.0 / samples).astype(jnp.bfloat16)
    root = math.sqrt(2.0) - 1.0

    def window(w, total):
        record = traces[w]
        parts = jnp.dot(record, table, preferred_element_type=jnp.float32)
        mean, alternate = parts[:, :part], parts[:, part:]
        for q in range(n_freq):
            rest = record[:, q * part : (q + 1) * part].astype(jnp.float32) - mean
            total = total + rest * rest
        total = total + n_freq * alternate * alternate
        own = traces[w, :, pl.ds(pl.multiple_of(f * part, part), part)].astype(jnp.float32)
        spectra[w] = own - mean + root * alternate
        return total

    total = lax.fori_loop(0, windows, window, jnp.zeros((channels, part), jnp.float32))
    energy = (0.5 * samples) * jnp.sum(total, axis=1, keepdims=True)
    inverse = lax.rsqrt(energy / (windows * samples) + 1e-05)

    pl.semaphore_wait(barrier, len(peers))

    def slot(row, col):
        return whole.at[row, pl.ds(pl.multiple_of(col * channels, channels), channels)]

    def forward(d):
        source = slot(i, lax.rem(j + n_col - d, n_col))
        copies = []
        for e in range(1, n_row):
            copy = pltpu.make_async_remote_copy(
                src_ref=source,
                dst_ref=source,
                send_sem=x_send.at[d, e - 1],
                recv_sem=x_recv.at[d, e - 1],
                device_id=row_peer(e),
                device_id_type=MESH,
            )
            copy.start()
            copies.append(copy)
        return copies

    z_copies, x_copies = [], []
    for d in range(n_col):
        target = lax.rem(j + d, n_col)
        for k in range(share):
            white = (spectra[target * share + k] * inverse).astype(jnp.bfloat16)
            if d == 0:
                whole[i, pl.ds(pl.multiple_of(j * channels, channels), channels), pl.ds(k * part, part)] = white
            else:
                blocks[d - 1, :, pl.ds(k * part, part)] = white
        if d == 0:
            x_copies += forward(0)
        else:
            copy = pltpu.make_async_remote_copy(
                src_ref=blocks.at[d - 1],
                dst_ref=slot(i, j),
                send_sem=z_send.at[d - 1],
                recv_sem=z_recv.at[d - 1],
                device_id=col_peer(d),
                device_id_type=MESH,
            )
            copy.start()
            z_copies.append(copy)
    nearest = sorted(range(1, n_col), key=lambda d: (min(d, n_col - d), d))
    for d in nearest:
        z_copies[d - 1].wait_recv()
        x_copies += forward(d)
    for copy in x_copies:
        copy.wait_recv()

    width = n_row * channels

    def own_rows(c):
        picked = []
        for s in range(n_freq // 2):
            first = (2 * s + c) * rows
            picked.append(whole[i, pl.ds(pl.multiple_of(first, rows), rows), :])
        return jnp.concatenate(picked, axis=0)

    a_copies, b_copies, c_copies = [], [], []
    order = list(range(1, n_col)) + [0]

    def stage_a(t):
        target = lax.rem(j + order[t], n_col)
        columns = jnp.concatenate(
            [whole[r, pl.ds(pl.multiple_of(target * channels, channels), channels), :] for r in range(n_row)],
            axis=0,
        )
        away = lax.dot_general(own_rows(1 - core), columns, NT, preferred_element_type=jnp.float32)
        send_a[t] = away.astype(jnp.bfloat16).reshape(2, rows, width)
        copy = pltpu.make_async_remote_copy(
            src_ref=send_a.at[t],
            dst_ref=recv_a.at[t],
            send_sem=a_send.at[t],
            recv_sem=a_recv.at[t],
            device_id=core_peer,
            device_id_type=MESH,
        )
        copy.start()
        a_copies.append(copy)
        near = lax.dot_general(own_rows(core), columns, NT, preferred_element_type=jnp.float32)
        keep_a[t % 2] = near.reshape(2, rows, width)

    def stage_b(t):
        a_copies[t].wait_recv()
        away = keep_a[t % 2, 1 - side] + recv_a[t, 1 - side].astype(jnp.float32)
        send_b[t] = away.astype(jnp.bfloat16)
        copy = pltpu.make_async_remote_copy(
            src_ref=send_b.at[t],
            dst_ref=recv_b.at[t],
            send_sem=b_send.at[t],
            recv_sem=b_recv.at[t],
            device_id=side_peer,
            device_id_type=MESH,
        )
        copy.start()
        b_copies.append(copy)
        keep_b[t % 2] = keep_a[t % 2, side] + recv_a[t, side].astype(jnp.float32)

    def stage_c(t):
        d = order[t]
        b_copies[t].wait_recv()
        value = keep_b[t % 2] + recv_b[t].astype(jnp.float32)
        if d == 0:
            keep_c[...] = value
            return
        send_c[d - 1] = value.astype(jnp.bfloat16)
        copy = pltpu.make_async_remote_copy(
            src_ref=send_c.at[d - 1],
            dst_ref=recv_c.at[d - 1],
            send_sem=c_send.at[d - 1],
            recv_sem=c_recv.at[d - 1],
            device_id=col_peer(d),
            device_id_type=MESH,
        )
        copy.start()
        c_copies.append(copy)

    for t in range(n_col + 2):
        if t < n_col:
            stage_a(t)
        if 1 <= t <= n_col:
            stage_b(t - 1)
        if t >= 2:
            stage_c(t - 2)

    value = keep_c[...]
    for d in range(1, n_col):
        c_copies[d - 1].wait_recv()
        value = value + recv_c[d - 1].astype(jnp.float32)
    value = value * (0.5 * samples / math.sqrt(windows * samples))
    for r in range(n_row):
        out[:, r, 0, :] = value[:, r * channels : (r + 1) * channels]
    for copy in z_copies + x_copies + a_copies + b_copies + c_copies:
        copy.wait_send()


def on_device(n_row, n_col, n_freq, traces):
    windows, channels, samples = traces.shape
    part = samples // n_freq
    depth = windows // n_col * part
    rows = n_col * channels // n_freq
    width = n_row * channels
    bf16, f32, dma = jnp.bfloat16, jnp.float32, pltpu.SemaphoreType.DMA
    return pl.pallas_call(
        functools.partial(kernel, n_row, n_col, n_freq),
        out_shape=jax.ShapeDtypeStruct((rows, n_row, 1, channels), f32),
        in_specs=[pl.BlockSpec(memory_space=pltpu.VMEM)],
        out_specs=pl.BlockSpec(memory_space=pltpu.VMEM),
        scratch_shapes=[
            pltpu.VMEM((windows, channels, part), f32),
            pltpu.VMEM((n_col - 1, channels, depth), bf16),
            pltpu.VMEM((n_row, n_col * channels, depth), bf16),
            pltpu.VMEM((n_col, 2, rows, width), bf16),
            pltpu.VMEM((2, 2, rows, width), f32),
            pltpu.VMEM((n_col, 2, rows, width), bf16),
            pltpu.VMEM((n_col, rows, width), bf16),
            pltpu.VMEM((2, rows, width), f32),
            pltpu.VMEM((n_col, rows, width), bf16),
            pltpu.VMEM((n_col - 1, rows, width), bf16),
            pltpu.VMEM((rows, width), f32),
            pltpu.VMEM((n_col - 1, rows, width), bf16),
            dma((n_col - 1,)),
            dma((n_col - 1,)),
            dma((n_col, n_row - 1)),
            dma((n_col, n_row - 1)),
            dma((n_col,)),
            dma((n_col,)),
            dma((n_col,)),
            dma((n_col,)),
            dma((n_col - 1,)),
            dma((n_col - 1,)),
        ],
        compiler_params=pltpu.CompilerParams(
            collective_id=0, has_side_effects=True, vmem_limit_bytes=56 * 1024 * 1024
        ),
    )(traces)


def solution(mesh):
    sizes = [mesh.shape[axis] for axis in ("row", "col", "freq")]
    return jax.shard_map(
        functools.partial(on_device, *sizes),
        mesh=mesh,
        in_specs=(P(None, ("row", "col"), None),),
        out_specs=P(("row", "freq"), None, "col", None),
        check_vma=False,
    )
```

```python
import functools
import math

import jax
import jax.numpy as jnp
from jax import lax
from jax.experimental import pallas as pl
from jax.experimental.pallas import tpu as pltpu
from jax.sharding import PartitionSpec as P

MESH = pl.DeviceIdType.MESH
NT = (((1,), (1,)), ((), ()))


def kernel(
    n_row, n_col, n_freq, given, out, traces, spectra, blocks, whole,
    send_a0, keep_a0, recv_a0, send_b0, keep_b0, recv_b0, send_c0, keep_c0, recv_c0,
    send_a1, keep_a1, recv_a1, send_b1, keep_b1, recv_b1, send_c1, keep_c1, recv_c1,
    z_send, z_recv, x_send, x_recv, a_send, a_recv, b_send, b_recv, c_send, c_recv, load,
):
    groups = (
        (send_a0, keep_a0, recv_a0, send_b0, keep_b0, recv_b0, send_c0, keep_c0, recv_c0),
        (send_a1, keep_a1, recv_a1, send_b1, keep_b1, recv_b1, send_c1, keep_c1, recv_c1),
    )
    windows, channels, samples = traces.shape
    part = samples // n_freq
    share = windows // n_col
    rows = n_col * channels // n_freq
    i, j, f = lax.axis_index("row"), lax.axis_index("col"), lax.axis_index("freq")
    core = lax.rem(f, 2)
    side = lax.div(f, 2)
    core_peer = (i, j, f + 1 - 2 * core)
    side_peer = (i, j, lax.rem(f + 2, n_freq))

    def col_peer(d):
        return (i, lax.rem(j + d, n_col), f)

    def row_peer(e):
        return (lax.rem(i + e, n_row), j, f)

    peers = [core_peer, side_peer]
    peers += [col_peer(d) for d in range(1, n_col)]
    peers += [row_peer(e) for e in range(1, n_row)]
    barrier = pltpu.get_barrier_semaphore()
    for peer in peers:
        pl.semaphore_signal(barrier, inc=1, device_id=peer, device_id_type=MESH)

    loads = []
    batch = windows // n_col
    for p in range(n_col):
        group = pl.ds(p * batch, batch)
        copy = pltpu.make_async_copy(given.at[group], traces.at[group], load.at[p])
        copy.start()
        loads.append(copy)

    time = lax.broadcasted_iota(jnp.int32, (samples, 2 * part), 0)
    lane = lax.broadcasted_iota(jnp.int32, (samples, 2 * part), 1)
    odd = jnp.logical_and(lane >= part, lax.rem(time + lane, 2) == 1)
    table = jnp.where(odd, -1.0 / samples, 1.0 / samples).astype(jnp.bfloat16)
    root = math.sqrt(2.0) - 1.0

    def window(w, total):
        record = traces[w]
        parts = jnp.dot(record, table, preferred_element_type=jnp.float32)
        mean, alternate = parts[:, :part], parts[:, part:]
        for q in range(n_freq):
            rest = record[:, q * part : (q + 1) * part].astype(jnp.float32) - mean
            total = total + rest * rest
        total = total + n_freq * alternate * alternate
        own = traces[w, :, pl.ds(pl.multiple_of(f * part, part), part)].astype(jnp.float32)
        spectra[w] = own - mean + root * alternate
        return total

    total = jnp.zeros((channels, part), jnp.float32)
    for p in range(n_col):
        loads[p].wait()
        total = lax.fori_loop(p * batch, (p + 1) * batch, window, total)
    energy = (0.5 * samples) * jnp.sum(total, axis=1, keepdims=True)
    inverse = lax.rsqrt(energy / (windows * samples) + 1e-05)

    pl.semaphore_wait(barrier, len(peers))

    chunks = math.gcd(share, 3)
    span = share // chunks * part

    def slot(row, col, c):
        return whole.at[
            row, pl.ds(pl.multiple_of(col * channels, channels), channels), pl.ds(c * span, span)
        ]

    def forward(d, c):
        source = slot(i, lax.rem(j + n_col - d, n_col), c)
        copies = []
        for e in range(1, n_row):
            copy = pltpu.make_async_remote_copy(
                src_ref=source,
                dst_ref=source,
                send_sem=x_send.at[c, d, e - 1],
                recv_sem=x_recv.at[c, d, e - 1],
                device_id=row_peer(e),
                device_id_type=MESH,
            )
            copy.start()
            copies.append(copy)
        return copies

    z_copies, x_copies = {}, []
    for c in range(chunks):
        for d in range(n_col):
            target = lax.rem(j + d, n_col)
            for k in range(c * share // chunks, (c + 1) * share // chunks):
                white = (spectra[target * share + k] * inverse).astype(jnp.bfloat16)
                lanes = pl.ds(k * part, part)
                if d == 0:
                    whole[i, pl.ds(pl.multiple_of(j * channels, channels), channels), lanes] = white
                else:
                    blocks[d - 1, :, lanes] = white
            if d == 0:
                x_copies += forward(0, c)
            else:
                copy = pltpu.make_async_remote_copy(
                    src_ref=blocks.at[d - 1, :, pl.ds(c * span, span)],
                    dst_ref=slot(i, j, c),
                    send_sem=z_send.at[c, d - 1],
                    recv_sem=z_recv.at[c, d - 1],
                    device_id=col_peer(d),
                    device_id_type=MESH,
                )
                copy.start()
                z_copies[c, d] = copy
    nearest = sorted(range(1, n_col), key=lambda d: (min(d, n_col - d), d))
    for c in range(chunks):
        for d in nearest:
            z_copies[c, d].wait_recv()
            x_copies += forward(d, c)
    z_copies = list(z_copies.values())

    def own_rows(c):
        picked = []
        for s in range(n_freq // 2):
            first = (2 * s + c) * rows
            picked.append(whole[i, pl.ds(pl.multiple_of(first, rows), rows), :])
        return jnp.concatenate(picked, axis=0)

    out_copies = []
    order = list(range(1, n_col)) + [0]

    def remote(source, target, send, receive, peer):
        copy = pltpu.make_async_remote_copy(
            src_ref=source,
            dst_ref=target,
            send_sem=send,
            recv_sem=receive,
            device_id=peer,
            device_id_type=MESH,
        )
        copy.start()
        out_copies.append(copy)
        return copy

    def run(g, t, stage):
        shifts = [0] if g == 0 else list(range(1, n_row))
        wide = len(shifts) * channels
        send_a, keep_a, recv_a, send_b, keep_b, recv_b, send_c, keep_c, recv_c = groups[g]
        d = order[t]
        if stage == 0:
            target = pl.ds(pl.multiple_of(lax.rem(j + d, n_col) * channels, channels), channels)
            columns = jnp.concatenate([whole[lax.rem(i + e, n_row), target, :] for e in shifts], axis=0)
            away = lax.dot_general(own_rows(1 - core), columns, NT, preferred_element_type=jnp.float32)
            send_a[t] = away.astype(jnp.bfloat16).reshape(2, rows, wide)
            a_copies[g, t] = remote(
                send_a.at[t], recv_a.at[t], a_send.at[g, t], a_recv.at[g, t], core_peer
            )
            near = lax.dot_general(own_rows(core), columns, NT, preferred_element_type=jnp.float32)
            keep_a[t % 2] = near.reshape(2, rows, wide)
        elif stage == 1:
            a_copies[g, t].wait_recv()
            away = keep_a[t % 2, 1 - side] + recv_a[t, 1 - side].astype(jnp.float32)
            send_b[t] = away.astype(jnp.bfloat16)
            b_copies[g, t] = remote(
                send_b.at[t], recv_b.at[t], b_send.at[g, t], b_recv.at[g, t], side_peer
            )
            keep_b[t % 2] = keep_a[t % 2, side] + recv_a[t, side].astype(jnp.float32)
        else:
            b_copies[g, t].wait_recv()
            value = keep_b[t % 2] + recv_b[t].astype(jnp.float32)
            if d == 0:
                keep_c[...] = value
                return
            send_c[d - 1] = value.astype(jnp.bfloat16)
            c_copies[g, d] = remote(
                send_c.at[d - 1], recv_c.at[d - 1], c_send.at[g, d - 1], c_recv.at[g, d - 1], col_peer(d)
            )

    a_copies, b_copies, c_copies = {}, {}, {}
    for g in range(2):
        if g == 1:
            for copy in x_copies:
                copy.wait_recv()
        for t in range(n_col + 2):
            if t < n_col:
                run(g, t, 0)
            if 1 <= t <= n_col:
                run(g, t - 1, 1)
            if t >= 2:
                run(g, t - 2, 2)

    for g in range(2):
        keep_c, recv_c = groups[g][7:]
        value = keep_c[...]
        for d in range(1, n_col):
            c_copies[g, d].wait_recv()
            value = value + recv_c[d - 1].astype(jnp.float32)
        value = value * (0.5 * samples / math.sqrt(windows * samples))
        for n, e in enumerate([0] if g == 0 else range(1, n_row)):
            place = pl.ds(pl.multiple_of(lax.rem(i + e, n_row) * channels, channels), channels)
            out[:, place] = value[:, n * channels : (n + 1) * channels]
    for copy in z_copies + x_copies + out_copies:
        copy.wait_send()


def on_device(n_row, n_col, n_freq, traces):
    windows, channels, samples = traces.shape
    part = samples // n_freq
    depth = windows // n_col * part
    rows = n_col * channels // n_freq
    chunks = math.gcd(windows // n_col, 3)
    bf16, f32, dma = jnp.bfloat16, jnp.float32, pltpu.SemaphoreType.DMA

    def tiles(width):
        return [
            pltpu.VMEM((n_col, 2, rows, width), bf16),
            pltpu.VMEM((2, 2, rows, width), f32),
            pltpu.VMEM((n_col, 2, rows, width), bf16),
            pltpu.VMEM((n_col, rows, width), bf16),
            pltpu.VMEM((2, rows, width), f32),
            pltpu.VMEM((n_col, rows, width), bf16),
            pltpu.VMEM((n_col - 1, rows, width), bf16),
            pltpu.VMEM((rows, width), f32),
            pltpu.VMEM((n_col - 1, rows, width), bf16),
        ]

    result = pl.pallas_call(
        functools.partial(kernel, n_row, n_col, n_freq),
        out_shape=jax.ShapeDtypeStruct((rows, n_row * channels), f32),
        in_specs=[pl.BlockSpec(memory_space=pl.ANY)],
        out_specs=pl.BlockSpec(memory_space=pltpu.VMEM),
        scratch_shapes=[
            pltpu.VMEM((windows, channels, samples), bf16),
            pltpu.VMEM((windows, channels, part), f32),
            pltpu.VMEM((n_col - 1, channels, depth), bf16),
            pltpu.VMEM((n_row, n_col * channels, depth), bf16),
            *tiles(channels),
            *tiles((n_row - 1) * channels),
            dma((chunks, n_col - 1)),
            dma((chunks, n_col - 1)),
            dma((chunks, n_col, n_row - 1)),
            dma((chunks, n_col, n_row - 1)),
            dma((2, n_col)),
            dma((2, n_col)),
            dma((2, n_col)),
            dma((2, n_col)),
            dma((2, n_col - 1)),
            dma((2, n_col - 1)),
            dma((n_col,)),
        ],
        compiler_params=pltpu.CompilerParams(
            collective_id=0, has_side_effects=True, vmem_limit_bytes=56 * 1024 * 1024
        ),
    )(traces)
    return result.reshape(rows, n_row, 1, channels)


def solution(mesh):
    sizes = [mesh.shape[axis] for axis in ("row", "col", "freq")]
    return jax.shard_map(
        functools.partial(on_device, *sizes),
        mesh=mesh,
        in_specs=(P(None, ("row", "col"), None),),
        out_specs=P(("row", "freq"), None, "col", None),
        check_vma=False,
    )
```

```python
import functools
import math

import jax
import jax.numpy as jnp
from jax import lax
from jax.experimental import pallas as pl
from jax.experimental.pallas import tpu as pltpu
from jax.sharding import PartitionSpec as P

MESH = pl.DeviceIdType.MESH
NT = (((1,), (1,)), ((), ()))


def kernel(
    n_row, n_col, n_freq, given, out, traces, spectra, blocks, whole,
    send_a0, keep_a0, recv_a0, send_b0, keep_b0, recv_b0, send_c0, keep_c0, recv_c0,
    send_a1, keep_a1, recv_a1, send_b1, keep_b1, recv_b1, send_c1, keep_c1, recv_c1,
    z_send, z_recv, x_send, x_recv, a_send, a_recv, b_send, b_recv, c_send, c_recv, load,
):
    groups = (
        (send_a0, keep_a0, recv_a0, send_b0, keep_b0, recv_b0, send_c0, keep_c0, recv_c0),
        (send_a1, keep_a1, recv_a1, send_b1, keep_b1, recv_b1, send_c1, keep_c1, recv_c1),
    )
    windows, channels, samples = traces.shape
    part = samples // n_freq
    share = windows // n_col
    rows = n_col * channels // n_freq
    i, j, f = lax.axis_index("row"), lax.axis_index("col"), lax.axis_index("freq")
    core = lax.rem(f, 2)
    side = lax.div(f, 2)
    core_peer = (i, j, f + 1 - 2 * core)
    side_peer = (i, j, lax.rem(f + 2, n_freq))

    def col_peer(d):
        return (i, lax.rem(j + d, n_col), f)

    def row_peer(e):
        return (lax.rem(i + e, n_row), j, f)

    peers = [core_peer, side_peer]
    peers += [col_peer(d) for d in range(1, n_col)]
    peers += [row_peer(e) for e in range(1, n_row)]
    barrier = pltpu.get_barrier_semaphore()
    for peer in peers:
        pl.semaphore_signal(barrier, inc=1, device_id=peer, device_id_type=MESH)

    loads = []
    batch = windows // n_col
    for p in range(n_col):
        group = pl.ds(p * batch, batch)
        copy = pltpu.make_async_copy(given.at[group], traces.at[group], load.at[p])
        copy.start()
        loads.append(copy)

    time = lax.broadcasted_iota(jnp.int32, (samples, 2 * part), 0)
    lane = lax.broadcasted_iota(jnp.int32, (samples, 2 * part), 1)
    odd = jnp.logical_and(lane >= part, lax.rem(time + lane, 2) == 1)
    table = jnp.where(odd, -1.0 / samples, 1.0 / samples).astype(jnp.bfloat16)
    root = math.sqrt(2.0) - 1.0

    def window(w, total):
        record = traces[w]
        parts = jnp.dot(record, table, preferred_element_type=jnp.float32)
        mean, alternate = parts[:, :part], parts[:, part:]
        for q in range(n_freq):
            rest = record[:, q * part : (q + 1) * part].astype(jnp.float32) - mean
            total = total + rest * rest
        total = total + n_freq * alternate * alternate
        own = traces[w, :, pl.ds(pl.multiple_of(f * part, part), part)].astype(jnp.float32)
        spectra[w] = own - mean + root * alternate
        return total

    total = jnp.zeros((channels, part), jnp.float32)
    for p in range(n_col):
        loads[p].wait()
        total = lax.fori_loop(p * batch, (p + 1) * batch, window, total)
    energy = (0.5 * samples) * jnp.sum(total, axis=1, keepdims=True)
    inverse = lax.rsqrt(energy / (windows * samples) + 1e-05)

    pl.semaphore_wait(barrier, len(peers))

    chunks = math.gcd(share, 3)
    span = share // chunks * part

    def slot(row, col, c):
        return whole.at[
            row, pl.ds(pl.multiple_of(col * channels, channels), channels), pl.ds(c * span, span)
        ]

    def forward(d, c):
        source = slot(i, lax.rem(j + n_col - d, n_col), c)
        copies = []
        for e in range(1, n_row):
            copy = pltpu.make_async_remote_copy(
                src_ref=source,
                dst_ref=source,
                send_sem=x_send.at[c, d, e - 1],
                recv_sem=x_recv.at[c, d, e - 1],
                device_id=row_peer(e),
                device_id_type=MESH,
            )
            copy.start()
            copies.append(copy)
        return copies

    z_copies, x_copies = {}, []
    for c in range(chunks):
        for d in range(n_col):
            target = lax.rem(j + d, n_col)
            for k in range(c * share // chunks, (c + 1) * share // chunks):
                white = (spectra[target * share + k] * inverse).astype(jnp.bfloat16)
                lanes = pl.ds(k * part, part)
                if d == 0:
                    whole[i, pl.ds(pl.multiple_of(j * channels, channels), channels), lanes] = white
                else:
                    blocks[d - 1, :, lanes] = white
            if d == 0:
                x_copies += forward(0, c)
            else:
                copy = pltpu.make_async_remote_copy(
                    src_ref=blocks.at[d - 1, :, pl.ds(c * span, span)],
                    dst_ref=slot(i, j, c),
                    send_sem=z_send.at[c, d - 1],
                    recv_sem=z_recv.at[c, d - 1],
                    device_id=col_peer(d),
                    device_id_type=MESH,
                )
                copy.start()
                z_copies[c, d] = copy
    nearest = sorted(range(1, n_col), key=lambda d: (min(d, n_col - d), d))
    for c in range(chunks):
        for d in nearest:
            z_copies[c, d].wait_recv()
            x_copies += forward(d, c)
    z_copies = list(z_copies.values())

    def own_rows(c):
        picked = []
        for s in range(n_freq // 2):
            first = (2 * s + c) * rows
            picked.append(whole[i, pl.ds(pl.multiple_of(first, rows), rows), :])
        return jnp.concatenate(picked, axis=0)

    out_copies = []
    order = list(range(1, n_col)) + [0]

    def remote(source, target, send, receive, peer):
        copy = pltpu.make_async_remote_copy(
            src_ref=source,
            dst_ref=target,
            send_sem=send,
            recv_sem=receive,
            device_id=peer,
            device_id_type=MESH,
        )
        copy.start()
        out_copies.append(copy)
        return copy

    def run(g, t, stage):
        shifts = [0] if g == 0 else list(range(1, n_row))
        wide = len(shifts) * channels
        send_a, keep_a, recv_a, send_b, keep_b, recv_b, send_c, keep_c, recv_c = groups[g]
        d = order[t]
        if stage == 0:
            target = pl.ds(pl.multiple_of(lax.rem(j + d, n_col) * channels, channels), channels)
            columns = jnp.concatenate([whole[lax.rem(i + e, n_row), target, :] for e in shifts], axis=0)
            away = lax.dot_general(own_rows(1 - core), columns, NT, preferred_element_type=jnp.float32)
            send_a[t] = away.astype(jnp.bfloat16).reshape(2, rows, wide)
            a_copies[g, t] = remote(
                send_a.at[t], recv_a.at[t], a_send.at[g, t], a_recv.at[g, t], core_peer
            )
            near = lax.dot_general(own_rows(core), columns, NT, preferred_element_type=jnp.float32)
            keep_a[t % slots] = near.reshape(2, rows, wide)
        elif stage == 1:
            a_copies[g, t].wait_recv()
            away = keep_a[t % slots, 1 - side] + recv_a[t, 1 - side].astype(jnp.float32)
            send_b[t] = away.astype(jnp.bfloat16)
            b_copies[g, t] = remote(
                send_b.at[t], recv_b.at[t], b_send.at[g, t], b_recv.at[g, t], side_peer
            )
            keep_b[t % slots] = keep_a[t % slots, side] + recv_a[t, side].astype(jnp.float32)
        else:
            b_copies[g, t].wait_recv()
            value = keep_b[t % slots] + recv_b[t].astype(jnp.float32)
            if d == 0:
                keep_c[...] = value
                return
            send_c[d - 1] = value.astype(jnp.bfloat16)
            c_copies[g, d] = remote(
                send_c.at[d - 1], recv_c.at[d - 1], c_send.at[g, d - 1], c_recv.at[g, d - 1], col_peer(d)
            )

    slots = keep_a0.shape[0]
    a_copies, b_copies, c_copies = {}, {}, {}
    for g in range(2):
        if g == 1:
            for copy in x_copies:
                copy.wait_recv()
        for t in range(n_col + 2 * slots):
            for stage in range(3):
                if 0 <= t - stage * (slots - 1) < n_col:
                    run(g, t - stage * (slots - 1), stage)

    for g in range(2):
        keep_c, recv_c = groups[g][7:]
        value = keep_c[...]
        for d in range(1, n_col):
            c_copies[g, d].wait_recv()
            value = value + recv_c[d - 1].astype(jnp.float32)
        value = value * (0.5 * samples / math.sqrt(windows * samples))
        for n, e in enumerate([0] if g == 0 else range(1, n_row)):
            place = pl.ds(pl.multiple_of(lax.rem(i + e, n_row) * channels, channels), channels)
            out[:, place] = value[:, n * channels : (n + 1) * channels]
    for copy in z_copies + x_copies + out_copies:
        copy.wait_send()


def on_device(n_row, n_col, n_freq, traces):
    windows, channels, samples = traces.shape
    part = samples // n_freq
    depth = windows // n_col * part
    rows = n_col * channels // n_freq
    chunks = math.gcd(windows // n_col, 3)
    slots = min(n_col, 4)
    bf16, f32, dma = jnp.bfloat16, jnp.float32, pltpu.SemaphoreType.DMA

    def tiles(width):
        return [
            pltpu.VMEM((n_col, 2, rows, width), bf16),
            pltpu.VMEM((slots, 2, rows, width), f32),
            pltpu.VMEM((n_col, 2, rows, width), bf16),
            pltpu.VMEM((n_col, rows, width), bf16),
            pltpu.VMEM((slots, rows, width), f32),
            pltpu.VMEM((n_col, rows, width), bf16),
            pltpu.VMEM((n_col - 1, rows, width), bf16),
            pltpu.VMEM((rows, width), f32),
            pltpu.VMEM((n_col - 1, rows, width), bf16),
        ]

    result = pl.pallas_call(
        functools.partial(kernel, n_row, n_col, n_freq),
        out_shape=jax.ShapeDtypeStruct((rows, n_row * channels), f32),
        in_specs=[pl.BlockSpec(memory_space=pl.ANY)],
        out_specs=pl.BlockSpec(memory_space=pltpu.VMEM),
        scratch_shapes=[
            pltpu.VMEM((windows, channels, samples), bf16),
            pltpu.VMEM((windows, channels, part), f32),
            pltpu.VMEM((n_col - 1, channels, depth), bf16),
            pltpu.VMEM((n_row, n_col * channels, depth), bf16),
            *tiles(channels),
            *tiles((n_row - 1) * channels),
            dma((chunks, n_col - 1)),
            dma((chunks, n_col - 1)),
            dma((chunks, n_col, n_row - 1)),
            dma((chunks, n_col, n_row - 1)),
            dma((2, n_col)),
            dma((2, n_col)),
            dma((2, n_col)),
            dma((2, n_col)),
            dma((2, n_col - 1)),
            dma((2, n_col - 1)),
            dma((n_col,)),
        ],
        compiler_params=pltpu.CompilerParams(
            collective_id=0, has_side_effects=True, vmem_limit_bytes=56 * 1024 * 1024
        ),
    )(traces)
    return result.reshape(rows, n_row, 1, channels)


def solution(mesh):
    sizes = [mesh.shape[axis] for axis in ("row", "col", "freq")]
    return jax.shard_map(
        functools.partial(on_device, *sizes),
        mesh=mesh,
        in_specs=(P(None, ("row", "col"), None),),
        out_specs=P(("row", "freq"), None, "col", None),
        check_vma=False,
    )
```

```python
import functools
import math

import jax
import jax.numpy as jnp
from jax import lax
from jax.experimental import pallas as pl
from jax.experimental.pallas import tpu as pltpu
from jax.sharding import PartitionSpec as P

MESH = pl.DeviceIdType.MESH
NT = (((1,), (1,)), ((), ()))


def kernel(
    n_row, n_col, n_freq, given, out, traces, spectra, blocks, whole,
    send_a0, keep_a0, recv_a0, send_b0, keep_b0, recv_b0, send_c0, keep_c0, recv_c0,
    send_a1, keep_a1, recv_a1, send_b1, keep_b1, recv_b1, send_c1, keep_c1, recv_c1,
    z_send, z_recv, x_send, x_recv, a_send, a_recv, b_send, b_recv, c_send, c_recv, load,
):
    groups = (
        (send_a0, keep_a0, recv_a0, send_b0, keep_b0, recv_b0, send_c0, keep_c0, recv_c0),
        (send_a1, keep_a1, recv_a1, send_b1, keep_b1, recv_b1, send_c1, keep_c1, recv_c1),
    )
    windows, channels, samples = traces.shape
    part = samples // n_freq
    share = windows // n_col
    rows = n_col * channels // n_freq
    i, j, f = lax.axis_index("row"), lax.axis_index("col"), lax.axis_index("freq")
    core = lax.rem(f, 2)
    side = lax.div(f, 2)
    core_peer = (i, j, f + 1 - 2 * core)
    side_peer = (i, j, lax.rem(f + 2, n_freq))

    def col_peer(d):
        return (i, lax.rem(j + d, n_col), f)

    def row_peer(e):
        return (lax.rem(i + e, n_row), j, f)

    peers = [core_peer, side_peer]
    peers += [col_peer(d) for d in range(1, n_col)]
    peers += [row_peer(e) for e in range(1, n_row)]
    barrier = pltpu.get_barrier_semaphore()
    for peer in peers:
        pl.semaphore_signal(barrier, inc=1, device_id=peer, device_id_type=MESH)

    loads = []
    batch = windows // n_col
    for p in range(n_col):
        group = pl.ds(p * batch, batch)
        copy = pltpu.make_async_copy(given.at[group], traces.at[group], load.at[p])
        copy.start()
        loads.append(copy)

    time = lax.broadcasted_iota(jnp.int32, (samples, 2 * part), 0)
    lane = lax.broadcasted_iota(jnp.int32, (samples, 2 * part), 1)
    odd = jnp.logical_and(lane >= part, lax.rem(time + lane, 2) == 1)
    table = jnp.where(odd, -1.0 / samples, 1.0 / samples).astype(jnp.bfloat16)
    root = math.sqrt(2.0) - 1.0

    def window(w, total):
        record = traces[w]
        parts = jnp.dot(record, table, preferred_element_type=jnp.float32)
        mean, alternate = parts[:, :part], parts[:, part:]
        for q in range(n_freq):
            rest = record[:, q * part : (q + 1) * part].astype(jnp.float32) - mean
            total = total + rest * rest
        total = total + n_freq * alternate * alternate
        own = traces[w, :, pl.ds(pl.multiple_of(f * part, part), part)].astype(jnp.float32)
        spectra[w] = own - mean + root * alternate
        return total

    total = jnp.zeros((channels, part), jnp.float32)
    for p in range(n_col):
        loads[p].wait()
        total = lax.fori_loop(p * batch, (p + 1) * batch, window, total)
    energy = (0.5 * samples) * jnp.sum(total, axis=1, keepdims=True)
    inverse = lax.rsqrt(energy / (windows * samples) + 1e-05)

    pl.semaphore_wait(barrier, len(peers))

    chunks = math.gcd(share, 3)
    span = share // chunks * part

    def slot(row, col, c):
        return whole.at[
            row, pl.ds(pl.multiple_of(col * channels, channels), channels), pl.ds(c * span, span)
        ]

    def forward(d, c):
        source = slot(i, lax.rem(j + n_col - d, n_col), c)
        copies = []
        for e in range(1, n_row):
            copy = pltpu.make_async_remote_copy(
                src_ref=source,
                dst_ref=source,
                send_sem=x_send.at[c, d, e - 1],
                recv_sem=x_recv.at[c, d, e - 1],
                device_id=row_peer(e),
                device_id_type=MESH,
            )
            copy.start()
            copies.append(copy)
        return copies

    z_copies, x_blocks = {}, {}
    nearest = sorted(range(1, n_col), key=lambda d: (min(d, n_col - d), d))

    def issue(d):
        target = lax.rem(j + d, n_col)
        for c in range(chunks):
            for k in range(c * share // chunks, (c + 1) * share // chunks):
                white = (spectra[target * share + k] * inverse).astype(jnp.bfloat16)
                lanes = pl.ds(k * part, part)
                if d == 0:
                    whole[i, pl.ds(pl.multiple_of(j * channels, channels), channels), lanes] = white
                else:
                    blocks[d - 1, :, lanes] = white
            if d == 0:
                x_blocks[0, c] = forward(0, c)
                continue
            copy = pltpu.make_async_remote_copy(
                src_ref=blocks.at[d - 1, :, pl.ds(c * span, span)],
                dst_ref=slot(i, j, c),
                send_sem=z_send.at[c, d - 1],
                recv_sem=z_recv.at[c, d - 1],
                device_id=col_peer(d),
                device_id_type=MESH,
            )
            copy.start()
            z_copies[c, d] = copy

    ahead = 2
    issue(nearest[0])
    issue(0)
    for n in range(1, len(nearest) + ahead):
        if n < len(nearest):
            issue(nearest[n])
        if n >= ahead:
            for c in range(chunks):
                d = nearest[n - ahead]
                z_copies[c, d].wait_recv()
                x_blocks[d, c] = forward(d, c)
    x_copies = [copy for copies in x_blocks.values() for copy in copies]
    z_copies = list(z_copies.values())

    def own_rows(c):
        picked = []
        for s in range(n_freq // 2):
            first = (2 * s + c) * rows
            picked.append(whole[i, pl.ds(pl.multiple_of(first, rows), rows), :])
        return jnp.concatenate(picked, axis=0)

    out_copies = []
    orders = [list(range(1, n_col)) + [0], [(n_col - d) % n_col for d in [0] + nearest]]

    def remote(source, target, send, receive, peer):
        copy = pltpu.make_async_remote_copy(
            src_ref=source,
            dst_ref=target,
            send_sem=send,
            recv_sem=receive,
            device_id=peer,
            device_id_type=MESH,
        )
        copy.start()
        out_copies.append(copy)
        return copy

    def run(g, t, stage):
        shifts = [0] if g == 0 else list(range(1, n_row))
        wide = len(shifts) * channels
        send_a, keep_a, recv_a, send_b, keep_b, recv_b, send_c, keep_c, recv_c = groups[g]
        d = orders[g][t]
        if stage == 0:
            if g == 1:
                for c in range(chunks):
                    for copy in x_blocks[(n_col - d) % n_col, c]:
                        copy.wait_recv()
            target = pl.ds(pl.multiple_of(lax.rem(j + d, n_col) * channels, channels), channels)
            columns = jnp.concatenate([whole[lax.rem(i + e, n_row), target, :] for e in shifts], axis=0)
            away = lax.dot_general(own_rows(1 - core), columns, NT, preferred_element_type=jnp.float32)
            send_a[t] = away.astype(jnp.bfloat16).reshape(2, rows, wide)
            a_copies[g, t] = remote(
                send_a.at[t], recv_a.at[t], a_send.at[g, t], a_recv.at[g, t], core_peer
            )
            near = lax.dot_general(own_rows(core), columns, NT, preferred_element_type=jnp.float32)
            keep_a[t % slots] = near.reshape(2, rows, wide)
        elif stage == 1:
            a_copies[g, t].wait_recv()
            away = keep_a[t % slots, 1 - side] + recv_a[t, 1 - side].astype(jnp.float32)
            send_b[t] = away.astype(jnp.bfloat16)
            b_copies[g, t] = remote(
                send_b.at[t], recv_b.at[t], b_send.at[g, t], b_recv.at[g, t], side_peer
            )
            keep_b[t % slots] = keep_a[t % slots, side] + recv_a[t, side].astype(jnp.float32)
        else:
            b_copies[g, t].wait_recv()
            value = keep_b[t % slots] + recv_b[t].astype(jnp.float32)
            if d == 0:
                keep_c[...] = value
                return
            send_c[d - 1] = value.astype(jnp.bfloat16)
            c_copies[g, d] = remote(
                send_c.at[d - 1], recv_c.at[d - 1], c_send.at[g, d - 1], c_recv.at[g, d - 1], col_peer(d)
            )

    slots = keep_a0.shape[0]
    a_copies, b_copies, c_copies = {}, {}, {}
    lead = slots - 1
    plans = [
        [
            (g, t - stage * lead, stage)
            for t in range(n_col + 2 * lead)
            for stage in range(3)
            if 0 <= t - stage * lead < n_col
        ]
        for g in range(2)
    ]
    early, late = plans[0], plans[1]
    if n_col <= slots:
        early = [step for step in plans[0] if step[2] < 2]
        late = [step for step in plans[1] if step[2] == 0]
        late += [step for step in plans[0] if step[2] == 2]
        late += [step for step in plans[1] if step[2] > 0]
    for step in early:
        run(*step)
    for step in late:
        run(*step)

    for g in range(2):
        keep_c, recv_c = groups[g][7:]
        value = keep_c[...]
        for d in range(1, n_col):
            c_copies[g, d].wait_recv()
            value = value + recv_c[d - 1].astype(jnp.float32)
        value = value * (0.5 * samples / math.sqrt(windows * samples))
        for n, e in enumerate([0] if g == 0 else range(1, n_row)):
            place = pl.ds(pl.multiple_of(lax.rem(i + e, n_row) * channels, channels), channels)
            out[:, place] = value[:, n * channels : (n + 1) * channels]
    for copy in z_copies + x_copies + out_copies:
        copy.wait_send()


def on_device(n_row, n_col, n_freq, traces):
    windows, channels, samples = traces.shape
    part = samples // n_freq
    depth = windows // n_col * part
    rows = n_col * channels // n_freq
    chunks = math.gcd(windows // n_col, 3)
    slots = min(n_col, 4)
    bf16, f32, dma = jnp.bfloat16, jnp.float32, pltpu.SemaphoreType.DMA

    def tiles(width):
        return [
            pltpu.VMEM((n_col, 2, rows, width), bf16),
            pltpu.VMEM((slots, 2, rows, width), f32),
            pltpu.VMEM((n_col, 2, rows, width), bf16),
            pltpu.VMEM((n_col, rows, width), bf16),
            pltpu.VMEM((slots, rows, width), f32),
            pltpu.VMEM((n_col, rows, width), bf16),
            pltpu.VMEM((n_col - 1, rows, width), bf16),
            pltpu.VMEM((rows, width), f32),
            pltpu.VMEM((n_col - 1, rows, width), bf16),
        ]

    result = pl.pallas_call(
        functools.partial(kernel, n_row, n_col, n_freq),
        out_shape=jax.ShapeDtypeStruct((rows, n_row * channels), f32),
        in_specs=[pl.BlockSpec(memory_space=pl.ANY)],
        out_specs=pl.BlockSpec(memory_space=pltpu.VMEM),
        scratch_shapes=[
            pltpu.VMEM((windows, channels, samples), bf16),
            pltpu.VMEM((windows, channels, part), f32),
            pltpu.VMEM((n_col - 1, channels, depth), bf16),
            pltpu.VMEM((n_row, n_col * channels, depth), bf16),
            *tiles(channels),
            *tiles((n_row - 1) * channels),
            dma((chunks, n_col - 1)),
            dma((chunks, n_col - 1)),
            dma((chunks, n_col, n_row - 1)),
            dma((chunks, n_col, n_row - 1)),
            dma((2, n_col)),
            dma((2, n_col)),
            dma((2, n_col)),
            dma((2, n_col)),
            dma((2, n_col - 1)),
            dma((2, n_col - 1)),
            dma((n_col,)),
        ],
        compiler_params=pltpu.CompilerParams(
            collective_id=0, has_side_effects=True, vmem_limit_bytes=56 * 1024 * 1024
        ),
    )(traces)
    return result.reshape(rows, n_row, 1, channels)


def solution(mesh):
    sizes = [mesh.shape[axis] for axis in ("row", "col", "freq")]
    return jax.shard_map(
        functools.partial(on_device, *sizes),
        mesh=mesh,
        in_specs=(P(None, ("row", "col"), None),),
        out_specs=P(("row", "freq"), None, "col", None),
        check_vma=False,
    )
```

```python
import functools
import math

import jax
import jax.numpy as jnp
from jax import lax
from jax.experimental import pallas as pl
from jax.experimental.pallas import tpu as pltpu
from jax.sharding import PartitionSpec as P

MESH = pl.DeviceIdType.MESH
NT = (((1,), (1,)), ((), ()))


def kernel(
    n_row, n_col, n_freq, given, out, traces, spectra, blocks, whole,
    send_a0, keep_a0, recv_a0, send_b0, keep_b0, recv_b0, send_c0, keep_c0, recv_c0,
    send_a1, keep_a1, recv_a1, send_b1, keep_b1, recv_b1, send_c1, keep_c1, recv_c1,
    z_send, z_recv, x_send, x_recv, a_send, a_recv, b_send, b_recv, c_send, c_recv, load,
):
    groups = (
        (send_a0, keep_a0, recv_a0, send_b0, keep_b0, recv_b0, send_c0, keep_c0, recv_c0),
        (send_a1, keep_a1, recv_a1, send_b1, keep_b1, recv_b1, send_c1, keep_c1, recv_c1),
    )
    windows, channels, samples = traces.shape
    part = samples // n_freq
    share = windows // n_col
    rows = n_col * channels // n_freq
    i, j, f = lax.axis_index("row"), lax.axis_index("col"), lax.axis_index("freq")
    core = lax.rem(f, 2)
    side = lax.div(f, 2)
    core_peer = (i, j, f + 1 - 2 * core)
    side_peer = (i, j, lax.rem(f + 2, n_freq))

    def col_peer(d):
        return (i, lax.rem(j + d, n_col), f)

    def row_peer(e):
        return (lax.rem(i + e, n_row), j, f)

    peers = [core_peer, side_peer]
    peers += [col_peer(d) for d in range(1, n_col)]
    peers += [row_peer(e) for e in range(1, n_row)]
    barrier = pltpu.get_barrier_semaphore()
    for peer in peers:
        pl.semaphore_signal(barrier, inc=1, device_id=peer, device_id_type=MESH)

    loads = []
    batch = windows // n_col
    for p in range(n_col):
        group = pl.ds(p * batch, batch)
        copy = pltpu.make_async_copy(given.at[group], traces.at[group], load.at[p])
        copy.start()
        loads.append(copy)

    time = lax.broadcasted_iota(jnp.int32, (samples, 2 * part), 0)
    lane = lax.broadcasted_iota(jnp.int32, (samples, 2 * part), 1)
    odd = jnp.logical_and(lane >= part, lax.rem(time + lane, 2) == 1)
    table = jnp.where(odd, -1.0 / samples, 1.0 / samples).astype(jnp.bfloat16)
    root = math.sqrt(2.0) - 1.0

    def window(w, total):
        record = traces[w]
        parts = jnp.dot(record, table, preferred_element_type=jnp.float32)
        mean, alternate = parts[:, :part], parts[:, part:]
        for q in range(n_freq):
            rest = record[:, q * part : (q + 1) * part].astype(jnp.float32) - mean
            total = total + rest * rest
        total = total + n_freq * alternate * alternate
        own = traces[w, :, pl.ds(pl.multiple_of(f * part, part), part)].astype(jnp.float32)
        spectra[w] = own - mean + root * alternate
        return total

    total = jnp.zeros((channels, part), jnp.float32)
    for p in range(n_col):
        loads[p].wait()
        total = lax.fori_loop(p * batch, (p + 1) * batch, window, total, unroll=True)
    energy = (0.5 * samples) * jnp.sum(total, axis=1, keepdims=True)
    inverse = lax.rsqrt(energy / (windows * samples) + 1e-05)

    pl.semaphore_wait(barrier, len(peers))

    chunks = math.gcd(share, 3)
    span = share // chunks * part

    def slot(row, col, c):
        return whole.at[
            row, pl.ds(pl.multiple_of(col * channels, channels), channels), pl.ds(c * span, span)
        ]

    def forward(d, c):
        source = slot(i, lax.rem(j + n_col - d, n_col), c)
        copies = []
        for e in range(1, n_row):
            copy = pltpu.make_async_remote_copy(
                src_ref=source,
                dst_ref=source,
                send_sem=x_send.at[c, d, e - 1],
                recv_sem=x_recv.at[c, d, e - 1],
                device_id=row_peer(e),
                device_id_type=MESH,
            )
            copy.start()
            copies.append(copy)
        return copies

    z_copies, x_blocks = {}, {}
    nearest = sorted(range(1, n_col), key=lambda d: (min(d, n_col - d), d))

    def issue(d):
        target = lax.rem(j + d, n_col)
        for c in range(chunks):
            for k in range(c * share // chunks, (c + 1) * share // chunks):
                white = (spectra[target * share + k] * inverse).astype(jnp.bfloat16)
                lanes = pl.ds(k * part, part)
                if d == 0:
                    whole[i, pl.ds(pl.multiple_of(j * channels, channels), channels), lanes] = white
                else:
                    blocks[d - 1, :, lanes] = white
            if d == 0:
                x_blocks[0, c] = forward(0, c)
                continue
            copy = pltpu.make_async_remote_copy(
                src_ref=blocks.at[d - 1, :, pl.ds(c * span, span)],
                dst_ref=slot(i, j, c),
                send_sem=z_send.at[c, d - 1],
                recv_sem=z_recv.at[c, d - 1],
                device_id=col_peer(d),
                device_id_type=MESH,
            )
            copy.start()
            z_copies[c, d] = copy

    ahead = 2
    issue(nearest[0])
    issue(0)
    for n in range(1, len(nearest) + ahead):
        if n < len(nearest):
            issue(nearest[n])
        if n >= ahead:
            for c in range(chunks):
                d = nearest[n - ahead]
                z_copies[c, d].wait_recv()
                x_blocks[d, c] = forward(d, c)
    x_copies = [copy for copies in x_blocks.values() for copy in copies]
    z_copies = list(z_copies.values())

    def own_rows(c):
        picked = []
        for s in range(n_freq // 2):
            first = (2 * s + c) * rows
            picked.append(whole[i, pl.ds(pl.multiple_of(first, rows), rows), :])
        return jnp.concatenate(picked, axis=0)

    out_copies = []
    orders = [list(range(1, n_col)) + [0], [(n_col - d) % n_col for d in [0] + nearest]]

    def remote(source, target, send, receive, peer):
        copy = pltpu.make_async_remote_copy(
            src_ref=source,
            dst_ref=target,
            send_sem=send,
            recv_sem=receive,
            device_id=peer,
            device_id_type=MESH,
        )
        copy.start()
        out_copies.append(copy)
        return copy

    def run(g, t, stage):
        shifts = [0] if g == 0 else list(range(1, n_row))
        wide = len(shifts) * channels
        send_a, keep_a, recv_a, send_b, keep_b, recv_b, send_c, keep_c, recv_c = groups[g]
        d = orders[g][t]
        if stage == 0:
            if g == 1:
                for c in range(chunks):
                    for copy in x_blocks[(n_col - d) % n_col, c]:
                        copy.wait_recv()
            target = pl.ds(pl.multiple_of(lax.rem(j + d, n_col) * channels, channels), channels)
            columns = jnp.concatenate([whole[lax.rem(i + e, n_row), target, :] for e in shifts], axis=0)
            away = lax.dot_general(own_rows(1 - core), columns, NT, preferred_element_type=jnp.float32)
            send_a[t] = away.astype(jnp.bfloat16).reshape(2, rows, wide)
            a_copies[g, t] = remote(
                send_a.at[t], recv_a.at[t], a_send.at[g, t], a_recv.at[g, t], core_peer
            )
            near = lax.dot_general(own_rows(core), columns, NT, preferred_element_type=jnp.float32)
            keep_a[t % slots] = near.reshape(2, rows, wide)
        elif stage == 1:
            a_copies[g, t].wait_recv()
            away = keep_a[t % slots, 1 - side] + recv_a[t, 1 - side].astype(jnp.float32)
            send_b[t] = away.astype(jnp.bfloat16)
            b_copies[g, t] = remote(
                send_b.at[t], recv_b.at[t], b_send.at[g, t], b_recv.at[g, t], side_peer
            )
            keep_b[t % slots] = keep_a[t % slots, side] + recv_a[t, side].astype(jnp.float32)
        else:
            b_copies[g, t].wait_recv()
            value = keep_b[t % slots] + recv_b[t].astype(jnp.float32)
            if d == 0:
                keep_c[...] = value
                return
            send_c[d - 1] = value.astype(jnp.bfloat16)
            c_copies[g, d] = remote(
                send_c.at[d - 1], recv_c.at[d - 1], c_send.at[g, d - 1], c_recv.at[g, d - 1], col_peer(d)
            )

    slots = keep_a0.shape[0]
    a_copies, b_copies, c_copies = {}, {}, {}
    lead = slots - 1
    plans = [
        [
            (g, t - stage * lead, stage)
            for t in range(n_col + 2 * lead)
            for stage in range(3)
            if 0 <= t - stage * lead < n_col
        ]
        for g in range(2)
    ]
    early, late = plans[0], plans[1]
    if n_col <= slots:
        early = [step for step in plans[0] if step[2] < 2]
        late = [step for step in plans[1] if step[2] == 0]
        late += [step for step in plans[0] if step[2] == 2]
        late += [step for step in plans[1] if step[2] > 0]
    for step in early:
        run(*step)
    for step in late:
        run(*step)

    for g in range(2):
        keep_c, recv_c = groups[g][7:]
        value = keep_c[...]
        for d in range(1, n_col):
            c_copies[g, d].wait_recv()
            value = value + recv_c[d - 1].astype(jnp.float32)
        value = value * (0.5 * samples / math.sqrt(windows * samples))
        for n, e in enumerate([0] if g == 0 else range(1, n_row)):
            place = pl.ds(pl.multiple_of(lax.rem(i + e, n_row) * channels, channels), channels)
            out[:, place] = value[:, n * channels : (n + 1) * channels]
    for copy in z_copies + x_copies + out_copies:
        copy.wait_send()


def on_device(n_row, n_col, n_freq, traces):
    windows, channels, samples = traces.shape
    part = samples // n_freq
    depth = windows // n_col * part
    rows = n_col * channels // n_freq
    chunks = math.gcd(windows // n_col, 3)
    slots = min(n_col, 4)
    bf16, f32, dma = jnp.bfloat16, jnp.float32, pltpu.SemaphoreType.DMA

    def tiles(width):
        return [
            pltpu.VMEM((n_col, 2, rows, width), bf16),
            pltpu.VMEM((slots, 2, rows, width), f32),
            pltpu.VMEM((n_col, 2, rows, width), bf16),
            pltpu.VMEM((n_col, rows, width), bf16),
            pltpu.VMEM((slots, rows, width), f32),
            pltpu.VMEM((n_col, rows, width), bf16),
            pltpu.VMEM((n_col - 1, rows, width), bf16),
            pltpu.VMEM((rows, width), f32),
            pltpu.VMEM((n_col - 1, rows, width), bf16),
        ]

    result = pl.pallas_call(
        functools.partial(kernel, n_row, n_col, n_freq),
        out_shape=jax.ShapeDtypeStruct((rows, n_row * channels), f32),
        in_specs=[pl.BlockSpec(memory_space=pl.ANY)],
        out_specs=pl.BlockSpec(memory_space=pltpu.VMEM),
        scratch_shapes=[
            pltpu.VMEM((windows, channels, samples), bf16),
            pltpu.VMEM((windows, channels, part), f32),
            pltpu.VMEM((n_col - 1, channels, depth), bf16),
            pltpu.VMEM((n_row, n_col * channels, depth), bf16),
            *tiles(channels),
            *tiles((n_row - 1) * channels),
            dma((chunks, n_col - 1)),
            dma((chunks, n_col - 1)),
            dma((chunks, n_col, n_row - 1)),
            dma((chunks, n_col, n_row - 1)),
            dma((2, n_col)),
            dma((2, n_col)),
            dma((2, n_col)),
            dma((2, n_col)),
            dma((2, n_col - 1)),
            dma((2, n_col - 1)),
            dma((n_col,)),
        ],
        compiler_params=pltpu.CompilerParams(
            collective_id=0, has_side_effects=True, vmem_limit_bytes=56 * 1024 * 1024
        ),
    )(traces)
    return result.reshape(rows, n_row, 1, channels)


def solution(mesh):
    sizes = [mesh.shape[axis] for axis in ("row", "col", "freq")]
    return jax.shard_map(
        functools.partial(on_device, *sizes),
        mesh=mesh,
        in_specs=(P(None, ("row", "col"), None),),
        out_specs=P(("row", "freq"), None, "col", None),
        check_vma=False,
    )
```
